512 devices in a mesh: dp: 32 (over z_lo, y), fac: 16 (over x, z_hi, core).
Axes of the slice: x: 4, y: 8, z: 8 (z_hi: 2, z_lo: 4; z = z_hi * 4 + z_lo), core: 2. Of those that a mesh axis runs over, the one named last changes fastest.
Arguments:
- activations: bfloat16 [2048, 5120], P('fac', 'dp'), may hold values from -6 to 6
- output_grads: bfloat16 [2048, 13824], P('fac', 'dp'), may hold values from -6 to 6
- input_prior: float32 [5120, 5120], P('fac', 'dp'), as said below
- gradient_prior: float32 [13824, 13824], P('fac', 'dp'), as said below
- input_inverse: bfloat16 [5120, 5120], P('fac', 'dp'), as said below
- gradient_inverse: bfloat16 [13824, 13824], P('fac', 'dp'), as said below
Outputs:
- input_factor: float32 [5120, 5120], P('fac', 'dp')
- gradient_factor: float32 [13824, 13824], P('fac', 'dp')
- preconditioned: bfloat16 [5120, 13824], P('fac', 'dp')
The draws below stay inside these ranges and needn't reach their ends.
Inputs may be any that keep to these rules, and one draw needn't show every extreme that they name: `input_prior`: symmetric. `gradient_prior`: symmetric. `input_inverse`: symmetric. `gradient_inverse`: symmetric.
All inputs are finite; a program needn't handle non-finite values.
Results may differ from the reference program's by a relative error of at most 0.0057.
Values may be sent and summed in bfloat16 or wider, within the bound.
No kernel may reach another device: no remote copies, remote signals or barrier semaphores. Data moves between devices by JAX's collectives and lax.ppermute only.
A program may use at most 64 MiB of HBM per device.

```python
import math
import jax
import jax.numpy as jnp

D = 5120
FF = 13824
TOKENS = 2048


def assemble(key, noise_part, lowest, highest, spread):
    matrix_order = noise_part.shape[0]
    log_diagonal = jax.random.uniform(key, (matrix_order,), jnp.float32, math.log(lowest), math.log(highest))
    symmetric_part = (noise_part + noise_part.T) * (spread / math.sqrt(2.0 * matrix_order))
    return symmetric_part + jnp.diag(jnp.exp(log_diagonal))


def base_noise(key, matrix_order):
    return jax.random.normal(key, (matrix_order, matrix_order), jnp.float32)


def draw_input_prior(key, part):
    key = jax.random.fold_in(key, 11)
    noise_part = base_noise(key, D)
    return assemble(jax.random.fold_in(key, 5), noise_part, 0.5, 2.0, 0.5)


def draw_gradient_prior(key, part):
    key = jax.random.fold_in(key, 12)
    noise_part = base_noise(key, FF)
    return assemble(jax.random.fold_in(key, 5), noise_part, 0.5, 2.0, 0.5)


def draw_input_inverse(key, part):
    key = jax.random.fold_in(key, 13)
    noise_part = base_noise(key, D)
    return assemble(jax.random.fold_in(key, 5), noise_part, 2.0, 8.0, 2.0).astype(jnp.bfloat16)


def draw_gradient_inverse(key, part):
    key = jax.random.fold_in(key, 14)
    noise_part = base_noise(key, FF)
    return assemble(jax.random.fold_in(key, 5), noise_part, 2.0, 8.0, 2.0).astype(jnp.bfloat16)


def shard_levels(key, shape, cuts, least, top_value):
    gain, own = 1.0, jax.random.fold_in(key, 6)
    for axis_at, parts in cuts:
        heights = jnp.exp(jax.random.uniform(jax.random.fold_in(own, axis_at), (parts,), jnp.float32, least / len(cuts), top_value / len(cuts)))
        gain = gain * jnp.repeat(heights, shape[axis_at] // parts).reshape([-1 if axis == axis_at else 1 for axis in range(len(shape))])
    return gain


def bell_draw(stream_key, shape, scale, most, cuts=(), dtype=jnp.bfloat16):
    entries = jax.random.normal(stream_key, shape, jnp.float32) * scale
    if len(cuts) > 0:
        entries = shard_levels(stream_key, shape, cuts, -0.22, 0.18) * entries
    return jnp.clip(entries, min=-most, max=most).astype(dtype)


def setup_inputs(seed: int = 0) -> dict:
    seeds = jax.random.split(jax.random.key(seed), 7)
    return {
        "activations": bell_draw(seeds[0], (TOKENS, D), 1.0, 6.0, ((0, 16), (1, 32))),
        "output_grads": bell_draw(seeds[1], (TOKENS, FF), 1.0, 6.0, ((0, 16), (1, 32))),
        "input_prior": draw_input_prior(jax.random.fold_in(seeds[6], 71), 0),
        "gradient_prior": draw_gradient_prior(jax.random.fold_in(seeds[6], 71), 0),
        "input_inverse": draw_input_inverse(jax.random.fold_in(seeds[6], 71), 0),
        "gradient_inverse": draw_gradient_inverse(jax.random.fold_in(seeds[6], 71), 0),
    }


decay_rate = 0.95


def reference(activations, output_grads, input_prior, gradient_prior, input_inverse, gradient_inverse):
    weight_new = (1.0 - decay_rate) / TOKENS
    input_factor = decay_rate * input_prior + weight_new * jnp.dot(activations.T, activations, preferred_element_type=jnp.float32)
    gradient_factor = decay_rate * gradient_prior + weight_new * jnp.dot(output_grads.T, output_grads, preferred_element_type=jnp.float32)
    left_side = jnp.dot(activations, input_inverse.T, preferred_element_type=jnp.float32).astype(jnp.bfloat16)
    right_side = jnp.dot(output_grads, gradient_inverse, preferred_element_type=jnp.float32).astype(jnp.bfloat16)
    product = jnp.dot(left_side.T, right_side, preferred_element_type=jnp.float32)
    preconditioned = (product / TOKENS).astype(jnp.bfloat16)
    return input_factor, gradient_factor, preconditioned
```

```python
import functools
import jax
import jax.numpy as jnp
from jax import lax
from jax.experimental import pallas as pl
from jax.experimental.pallas import tpu as pltpu
from jax.sharding import Mesh, PartitionSpec as P

decay_rate = 0.95
VMEM = pl.BlockSpec(memory_space=pltpu.VMEM)
f32, bf16 = jnp.float32, jnp.bfloat16
shape = jax.ShapeDtypeStruct
AXES = ("zg", "p", "y", "xh", "xl", "w", "core")
SIZES = (2, 2, 8, 2, 2, 2, 2)
X = ("xh", "xl")
PANELS = 4
RING = 8


def device(zg, p, y, xh, xl, w, core):
    n = 0
    for size, at in zip(SIZES, (zg, p, y, xh, xl, w, core)):
        n = n * size + at
    return n


def coordinates():
    for n in range(512):
        out = []
        for size in SIZES[::-1]:
            out.append(n % size)
            n //= size
        yield out[::-1]


def panel_perm(flip):
    return [
        (
            device(zg, p, y, xh, xl, w, core),
            device(xh ^ flip, xl, PANELS * w + y % PANELS, zg, p, y // PANELS, core),
        )
        for zg, p, y, xh, xl, w, core in coordinates()
    ]


def piece_perm():
    return [
        (
            device(zg, p, y, xh, xl, w, core),
            device(xh, p, PANELS * w + y % PANELS, zg, xl, y // PANELS, core),
        )
        for zg, p, y, xh, xl, w, core in coordinates()
    ]


def column_perm():
    return [
        (
            device(zg, p, y, xh, xl, w, core),
            device(zg, p, y, xh, xl, w, core) if xl == p else device(zg, 1 - p, y, xh, 1 - xl, w, core),
        )
        for zg, p, y, xh, xl, w, core in coordinates()
    ]


def swap(x, axis):
    return lax.ppermute(x, axis, [(0, 1), (1, 0)])


def shift(x, axis, size, by):
    return lax.ppermute(x, axis, [(i, (i + by) % size) for i in range(size)])


def after(x, *others):
    return lax.optimization_barrier((x, *others))[0]


def dot(a, b, dims):
    return lax.dot_general(a, b, (dims, ((), ())), preferred_element_type=f32)


def call(kernel, out, flops, *args, scratch=()):
    size = sum(a.size * a.dtype.itemsize for a in (*args, *jax.tree.leaves(out)))
    return pl.pallas_call(
        kernel,
        out_shape=out,
        in_specs=[VMEM] * len(args),
        out_specs=jax.tree.map(lambda _: VMEM, out),
        scratch_shapes=list(scratch),
        compiler_params=pltpu.CompilerParams(vmem_limit_bytes=24 * 1024 * 1024),
        cost_estimate=pl.CostEstimate(flops=flops, bytes_accessed=size, transcendentals=0),
    )(*args)


def packed_shape(da, dg, h):
    return dg + da // 2, -(-dg * h // 128) * 128


def small_at(da, dg, h):
    lane = -(-da * h // 128) * 128
    return [
        (slice(i * da // 2, (i + 1) * da // 2), slice(dg, dg + da // 2), slice(i * lane, i * lane + da * h))
        for i in range(2)
    ]


def pack_kernel(small, big, out):
    da, dg = small.shape[0], big.shape[0]
    h = big.shape[1] // dg
    out[...] = jnp.zeros_like(out)
    out[:dg, : big.shape[1]] = big[...]
    for rows, to, lanes in small_at(da, dg, h):
        out[to, lanes] = small[rows, :]


def sides_kernel(da, dg, h, *refs):
    ring, inverses = refs[: RING + 1], refs[RING + 1 : RING + 5]
    rows, own, s1, s2, s3, acc = refs[RING + 5 :]
    core, zg, p, y = (lax.axis_index(a) for a in ("core", "zg", "p", "y"))
    x = 2 * lax.axis_index("xh") + lax.axis_index("xl")
    width, n = own.shape[1:]
    for offset, ref in zip((0, -1, 1, -2, 2, -3, 3), ring):
        at = lax.rem(y + offset + RING, RING)
        for slot in range(2):
            rows[at, lax.bitwise_xor(zg, slot)] = ref[slot]
    for slot in range(2):
        rows[lax.rem(y + 4, RING), lax.bitwise_xor(zg, slot)] = ring[RING - 1 + slot][...]
    big = [ref[:dg, : dg * h] for ref in inverses]
    small = [
        jnp.concatenate([ref[at, lanes] for _, at, lanes in small_at(da, dg, h)], 0) for ref in inverses
    ]
    for w in range(2):

        def panel(first, lo, hi):
            return jnp.concatenate(
                [
                    jnp.concatenate([rows[PANELS * w + first + m, xh, lo:hi, :] for m in range(h)], 0)
                    for xh in range(2)
                ],
                1,
            )

        for lo, hi, blocks in ((0, da, small), (da, width, big)):
            mine, other = panel(core * h, lo, hi), panel((1 - core) * h, lo, hi)
            for q in range(2):
                total = dot(blocks[2 * q], mine, ((1,), (0,))) + dot(blocks[2 * q + 1], other, ((1,), (0,)))
                for xh in range(2):
                    acc[2 * xh + lax.bitwise_xor(p, q), w, lo:hi, :] = total[:, xh * n : (xh + 1) * n]
    own[...] = acc[x]
    for ahead, ref in enumerate((s1, s2, s3)):
        ref[...] = acc[lax.rem(x + ahead + 1, 4)].astype(ref.dtype)


def first_sum_kernel(da, own, r1, r2, r3, keep, send):
    w = lax.axis_index("w")
    dg = own.shape[1] - da
    keep[...] = ((own[...] + r1[...].astype(f32)) + r2[...].astype(f32)) + r3[...].astype(f32)
    for t in range(2):
        send[t * dg : (t + 1) * dg, :] = keep[t, da:, :].astype(send.dtype)
    send[2 * dg :, :] = keep[1 - w, :da, :].astype(send.dtype)


def second_sum_kernel(da, keep, got, left, right):
    w = lax.axis_index("w")
    dg = right.shape[1]
    for t in range(2):
        right[t] = (keep[t, da:, :] + got[t * dg : (t + 1) * dg, :].astype(f32)).astype(right.dtype)
    left[...] = (keep[w, :da, :] + got[2 * dg :, :].astype(f32)).astype(left.dtype)


def factor_kernel(da, dg, h, weight, rows, cols, ip, gp, i_own, g_own, keep, send):
    core, p, w = (lax.axis_index(a) for a in ("core", "p", "w"))
    keep[...] = jnp.zeros_like(keep)
    send[...] = jnp.zeros_like(send)

    def panel(k, lo, hi):
        return jnp.concatenate([rows[PANELS * t + k, xh, lo:hi, :] for xh in range(2) for t in range(2)], 1)

    def columns(xl, lo, hi):
        return jnp.concatenate(
            [cols[2 * xh + xl, lax.bitwise_xor(w, t), lo:hi, :] for xh in range(2) for t in range(2)], 1
        )

    for lo, hi, prior, own in ((0, da, ip, i_own), (da, da + dg, gp, g_own)):
        n = hi - lo
        here, there = columns(p, lo, hi), columns(1 - p, lo, hi)
        for m in range(h):
            at = slice(m * n, (m + 1) * n)
            parts = [
                weight * dot(c, panel(first * h + m, lo, hi), ((1,), (1,)))
                for first in (core, 1 - core)
                for c in (here, there)
            ]
            own[:, at] = decay_rate * prior[:, at] + parts[0]
            for ref, part in ((keep, parts[1]), (send.at[0], parts[2]), (send.at[1], parts[3])):
                if lo:
                    ref[:dg, at] = part.astype(ref.dtype)
                else:
                    for src, to, lanes in small_at(da, dg, h):
                        lane = slice(lanes.start + m * n, lanes.start + (m + 1) * n)
                        ref[to, lane] = part[src, :].astype(ref.dtype)


def factor_sum_kernel(da, dg, h, i_own, g_own, got, last, i_out, g_out):
    def total(at, lanes):
        return got[0, at, lanes].astype(f32) + last[at, lanes].astype(f32)

    g_out[...] = g_own[...] + total(slice(0, dg), slice(0, dg * h))
    for src, at, lanes in small_at(da, dg, h):
        i_out[src, :] = i_own[src, :] + total(at, lanes)


def product_kernel(h, scale, left, right, r1, r2, r3, own, keep, send, held):
    core, p = lax.axis_index("core"), lax.axis_index("p")
    x = 2 * lax.axis_index("xh") + lax.axis_index("xl")
    n = left.shape[1]
    for behind, ref in enumerate((right, r1, r2, r3)):
        held[lax.rem(x - behind + 4, 4)] = ref[...]

    def columns(xl):
        return jnp.concatenate([held[2 * xh + xl, t] for xh in range(2) for t in range(2)], 1)

    here, there = columns(p), columns(1 - p)
    for first, outs in ((1 - core, (send.at[0], send.at[1])), (core, (own, keep))):
        for m in range(h):
            panel = jnp.concatenate([left[PANELS * b + first * h + m] for b in range(4)], 1)
            for c, ref in zip((here, there), outs):
                ref[m * n : (m + 1) * n, :] = (dot(panel, c, ((1,), (1,))) * scale).astype(ref.dtype)


def local(activations, output_grads, input_prior, gradient_prior, input_inverse, gradient_inverse):
    da, dg = activations.shape[1], output_grads.shape[1]
    width, block = da + dg, activations.shape[0]
    h = input_prior.shape[0] // da
    tokens = block * 16
    work = 2 * tokens * h * (da * da + dg * dg)
    pair = (2, width, block)
    pack = packed_shape(da, dg, h)

    x = jnp.concatenate([activations.T, output_grads.T], 0)
    u = jnp.stack([lax.ppermute(x, AXES, panel_perm(j)) for j in range(2)])
    up, down = [u], [u]
    for _ in range(3):
        up.append(shift(up[-1], "y", RING, 1))
        down.append(shift(down[-1], "y", RING, -1))
    ring = [u, up[1], down[1], up[2], down[2], up[3], down[3]]
    ring += [shift(up[3][0], "y", RING, 1), shift(down[3][1], "y", RING, -1)]

    inverse = call(
        pack_kernel, shape(pack, bf16), 0, after(input_inverse.T, x), gradient_inverse.T
    )
    inverse = after(inverse, u)
    inverse_z = swap(inverse, "p")
    inverses = [inverse, swap(inverse, "core"), inverse_z, swap(inverse_z, "core")]

    col = lax.ppermute(after(x, u), AXES, column_perm())
    cols = lax.all_gather(jnp.stack([col, swap(col, "w")]), X, axis=0, tiled=False)

    rows, own, *ahead = call(
        functools.partial(sides_kernel, da, dg, h),
        (shape((RING, *pair), bf16), shape(pair, f32)) + (shape(pair, bf16),) * 3,
        work, *ring, *inverses,
        scratch=[pltpu.VMEM((4, *pair), f32)],
    )
    got = [shift(part, X, 4, i + 1) for i, part in enumerate(ahead)]
    keep, send = call(
        functools.partial(first_sum_kernel, da),
        (shape(pair, f32), shape((2 * dg + da, block), bf16)),
        0, own, *got,
    )
    left, right = call(
        functools.partial(second_sum_kernel, da),
        (shape((da, block), bf16), shape((2, dg, block), bf16)),
        0, keep, swap(send, "w"),
    )
    piece = lax.ppermute(left, AXES, piece_perm())
    rights = [shift(right, X, 4, i + 1) for i in range(3)]

    i_own, g_own, f_keep, f_send = call(
        functools.partial(factor_kernel, da, dg, h, (1.0 - decay_rate) / tokens),
        (shape((da, da * h), f32), shape((dg, dg * h), f32), shape(pack, f32), shape((2, *pack), bf16)),
        work, rows, cols, input_prior.T, gradient_prior.T,
    )
    f_got = swap(f_send, "core")
    f_mid = after((f_keep + f_got[1].astype(f32)).astype(bf16), left)
    f_last = swap(f_mid, "p")
    input_factor, gradient_factor = call(
        functools.partial(factor_sum_kernel, da, dg, h),
        (shape((da, da * h), f32), shape((dg, dg * h), f32)),
        0, i_own, g_own, f_got, f_last,
    )

    pieces = jnp.broadcast_to(after(piece, f_mid), (16, *piece.shape))
    lefts = lax.all_to_all(pieces, ("zg", "y"), 0, 0, tiled=True)
    lefts = after(lefts, f_last)
    p_own, p_keep, p_send = call(
        functools.partial(product_kernel, h, 1.0 / tokens),
        (shape((da * h, dg), f32), shape((da * h, dg), f32), shape((2, da * h, dg), bf16)),
        2 * tokens * h * da * dg, lefts, right, *rights,
        scratch=[pltpu.VMEM((4, 2, dg, block), bf16)],
    )
    p_got = swap(p_send, "core")
    p_last = swap((p_keep + p_got[1].astype(f32)).astype(bf16), "p")
    preconditioned = (p_own + p_got[0].astype(f32) + p_last.astype(f32)).astype(bf16)
    return input_factor.T, gradient_factor.T, preconditioned


def solution(mesh):
    split = Mesh(mesh.devices.reshape(SIZES), AXES)
    placed = P(("xh", "xl", "w", "core"), ("zg", "p", "y"))
    return jax.shard_map(
        local,
        mesh=split,
        in_specs=(placed,) * 6,
        out_specs=(placed,) * 3,
        check_vma=False,
    )
```

```python
import functools
import jax
import jax.numpy as jnp
from jax import lax
from jax.experimental import pallas as pl
from jax.experimental.pallas import tpu as pltpu
from jax.sharding import Mesh, PartitionSpec as P

decay_rate = 0.95
VMEM = pl.BlockSpec(memory_space=pltpu.VMEM)
f32, bf16 = jnp.float32, jnp.bfloat16
shape = jax.ShapeDtypeStruct
AXES = ("zg", "p", "y", "xh", "xl", "w", "core")
SIZES = (2, 2, 8, 2, 2, 2, 2)
X = ("xh", "xl")
PANELS = 4
RING = 8


def device(zg, p, y, xh, xl, w, core):
    n = 0
    for size, at in zip(SIZES, (zg, p, y, xh, xl, w, core)):
        n = n * size + at
    return n


def coordinates():
    for n in range(512):
        out = []
        for size in SIZES[::-1]:
            out.append(n % size)
            n //= size
        yield out[::-1]


def panel_perm(flip):
    return [
        (
            device(zg, p, y, xh, xl, w, core),
            device(xh ^ flip, w, PANELS * (xl ^ zg) + y % PANELS, zg, p, y // PANELS, core),
        )
        for zg, p, y, xh, xl, w, core in coordinates()
    ]


def piece_perm():
    return [
        (
            device(zg, p, y, xh, xl, w, core),
            device(xh, p, PANELS * (xl ^ zg) + y % PANELS, zg, w, y // PANELS, core),
        )
        for zg, p, y, xh, xl, w, core in coordinates()
    ]


def column_perm():
    return [
        (
            device(zg, p, y, xh, xl, w, core),
            device(zg, w, y, xh, xl, p, core),
        )
        for zg, p, y, xh, xl, w, core in coordinates()
    ]


def swap(x, axis):
    return lax.ppermute(x, axis, [(0, 1), (1, 0)])


def shift(x, axis, size, by):
    return lax.ppermute(x, axis, [(i, (i + by) % size) for i in range(size)])


def after(x, *others):
    return lax.optimization_barrier((x, *others))[0]


def dot(a, b, dims):
    return lax.dot_general(a, b, (dims, ((), ())), preferred_element_type=f32)


def call(kernel, out, flops, *args, scratch=()):
    size = sum(a.size * a.dtype.itemsize for a in (*args, *jax.tree.leaves(out)))
    return pl.pallas_call(
        kernel,
        out_shape=out,
        in_specs=[VMEM] * len(args),
        out_specs=jax.tree.map(lambda _: VMEM, out),
        scratch_shapes=list(scratch),
        compiler_params=pltpu.CompilerParams(vmem_limit_bytes=16 * 1024 * 1024),
        cost_estimate=pl.CostEstimate(flops=flops, bytes_accessed=size, transcendentals=0),
    )(*args)


def packed_shape(da, dg, h):
    return dg + da // 2, -(-dg * h // 128) * 128


def small_at(da, dg, h):
    lane = -(-da * h // 128) * 128
    return [
        (slice(i * da // 2, (i + 1) * da // 2), slice(dg, dg + da // 2), slice(i * lane, i * lane + da * h))
        for i in range(2)
    ]


def pack_kernel(small, big, out):
    da, dg = small.shape[0], big.shape[0]
    h = big.shape[1] // dg
    out[...] = jnp.zeros_like(out)
    out[:dg, : big.shape[1]] = big[...]
    for rows, to, lanes in small_at(da, dg, h):
        out[to, lanes] = small[rows, :]


def sides_kernel(da, dg, h, *refs):
    ring, inverses = refs[: RING + 1], refs[RING + 1 : RING + 5]
    rows, own, send, acc = refs[RING + 5 :]
    core, zg, p, y = (lax.axis_index(a) for a in ("core", "zg", "p", "y"))
    group = lax.axis_index("xh")
    x = 2 * group + lax.axis_index("xl")
    width, n = own.shape[1:]

    def place(offset):
        return lax.bitwise_xor(lax.rem(y + offset + RING, RING), PANELS * group)

    for offset, ref in zip((0, -1, 1, -2, 2, -3, 3), ring):
        at = place(offset)
        for slot in range(2):
            rows[at, lax.bitwise_xor(zg, slot)] = ref[slot]
    for slot in range(2):
        rows[place(4), lax.bitwise_xor(zg, slot)] = ring[RING - 1 + slot][...]
    big = [ref[:dg, : dg * h] for ref in inverses]
    small = [
        jnp.concatenate([ref[at, lanes] for _, at, lanes in small_at(da, dg, h)], 0) for ref in inverses
    ]
    for xl in range(2):

        def panel(first, lo, hi):
            return jnp.concatenate(
                [
                    jnp.concatenate([rows[PANELS * xl + first + m, xh, lo:hi, :] for m in range(h)], 0)
                    for xh in range(2)
                ],
                1,
            )

        for lo, hi, blocks in ((0, da, small), (da, width, big)):
            mine, other = panel(core * h, lo, hi), panel((1 - core) * h, lo, hi)
            for q in range(2):
                total = dot(blocks[2 * q], mine, ((1,), (0,))) + dot(blocks[2 * q + 1], other, ((1,), (0,)))
                for xh in range(2):
                    acc[2 * xh + xl, lax.bitwise_xor(p, q), lo:hi, :] = total[:, xh * n : (xh + 1) * n]
    own[...] = acc[x]
    send[...] = acc[...].astype(send.dtype)


def first_sum_kernel(da, own, got, keep, send):
    w = lax.axis_index("w")
    x = 2 * lax.axis_index("xh") + lax.axis_index("xl")
    dg = own.shape[1] - da
    total = own[...]
    for i in range(1, 4):
        total = total + got[lax.rem(x + i, 4)].astype(f32)
    keep[...] = total
    for t in range(2):
        send[t * dg : (t + 1) * dg, :] = keep[t, da:, :].astype(send.dtype)
    send[2 * dg :, :] = keep[1 - w, :da, :].astype(send.dtype)


def second_sum_kernel(da, keep, got, left, right):
    w = lax.axis_index("w")
    dg = right.shape[1]
    for t in range(2):
        right[t] = (keep[t, da:, :] + got[t * dg : (t + 1) * dg, :].astype(f32)).astype(right.dtype)
    left[...] = (keep[w, :da, :] + got[2 * dg :, :].astype(f32)).astype(left.dtype)


def factor_kernel(da, dg, h, weight, rows, c0, c1, c2, c3, ip, gp, i_own, g_own, keep, send, held):
    core, p, w = (lax.axis_index(a) for a in ("core", "p", "w"))
    x = 2 * lax.axis_index("xh") + lax.axis_index("xl")
    for behind, ref in enumerate((c0, c1, c2, c3)):
        held[lax.rem(x - behind + 4, 4)] = ref[...]
    keep[...] = jnp.zeros_like(keep)
    send[...] = jnp.zeros_like(send)

    def panel(k, lo, hi):
        return jnp.concatenate([rows[PANELS * xl + k, xh, lo:hi, :] for xh in range(2) for xl in range(2)], 1)

    def columns(q, lo, hi):
        return jnp.concatenate([held[token, lax.bitwise_xor(q, w), lo:hi, :] for token in range(4)], 1)

    for lo, hi, prior, own in ((0, da, ip, i_own), (da, da + dg, gp, g_own)):
        n = hi - lo
        here, there = columns(p, lo, hi), columns(1 - p, lo, hi)
        for m in range(h):
            at = slice(m * n, (m + 1) * n)
            parts = [
                weight * dot(c, panel(first * h + m, lo, hi), ((1,), (1,)))
                for first in (core, 1 - core)
                for c in (here, there)
            ]
            own[:, at] = decay_rate * prior[:, at] + parts[0]
            for ref, part in ((keep, parts[1]), (send.at[0], parts[2]), (send.at[1], parts[3])):
                if lo:
                    ref[:dg, at] = part.astype(ref.dtype)
                else:
                    for src, to, lanes in small_at(da, dg, h):
                        lane = slice(lanes.start + m * n, lanes.start + (m + 1) * n)
                        ref[to, lane] = part[src, :].astype(ref.dtype)


def factor_sum_kernel(da, dg, h, i_own, g_own, got, last, i_out, g_out):
    def total(at, lanes):
        return got[0, at, lanes].astype(f32) + last[at, lanes].astype(f32)

    g_out[...] = g_own[...] + total(slice(0, dg), slice(0, dg * h))
    for src, at, lanes in small_at(da, dg, h):
        i_out[src, :] = i_own[src, :] + total(at, lanes)


def product_kernel(h, scale, left, right, r1, r2, r3, own, keep, send, held):
    core, p, group = lax.axis_index("core"), lax.axis_index("p"), lax.axis_index("xh")
    x = 2 * group + lax.axis_index("xl")
    n = left.shape[1]
    for behind, ref in enumerate((right, r1, r2, r3)):
        held[lax.rem(x - behind + 4, 4)] = ref[...]

    def columns(q):
        return jnp.concatenate([held[token, q] for token in range(4)], 1)

    def panel(k):
        return jnp.concatenate(
            [left[2 * PANELS * xh + PANELS * lax.bitwise_xor(xl, group) + k] for xh in range(2) for xl in range(2)], 1
        )

    here, there = columns(p), columns(1 - p)
    for first, outs in ((1 - core, (send.at[0], send.at[1])), (core, (own, keep))):
        for m in range(h):
            part = panel(first * h + m)
            for c, ref in zip((here, there), outs):
                ref[m * n : (m + 1) * n, :] = (dot(part, c, ((1,), (1,))) * scale).astype(ref.dtype)


def local(activations, output_grads, input_prior, gradient_prior, input_inverse, gradient_inverse):
    da, dg = activations.shape[1], output_grads.shape[1]
    width, block = da + dg, activations.shape[0]
    h = input_prior.shape[0] // da
    tokens = block * 16
    work = 2 * tokens * h * (da * da + dg * dg)
    pair = (2, width, block)
    pack = packed_shape(da, dg, h)

    x = jnp.concatenate([activations.T, output_grads.T], 0)
    inverse = call(pack_kernel, shape(pack, bf16), 0, after(input_inverse.T, x), gradient_inverse.T)
    first, second, col, inverse_c = lax.optimization_barrier(
        (
            lax.ppermute(x, AXES, panel_perm(0)),
            lax.ppermute(x, AXES, panel_perm(1)),
            lax.ppermute(x, AXES, column_perm()),
            swap(inverse, "core"),
        )
    )
    u = jnp.stack([first, second])
    up, down = [u], [u]
    for _ in range(3):
        up.append(shift(up[-1], "y", RING, 1))
        down.append(shift(down[-1], "y", RING, -1))
    ring = [u, up[1], down[1], up[2], down[2], up[3], down[3]]
    ring += [shift(up[3][0], "y", RING, 1), shift(down[3][1], "y", RING, -1)]

    inverse_z = swap(after(inverse, up[1], down[1]), "p")
    inverse_zc = swap(after(inverse_z, up[3], down[3]), "core")

    rows, own, send = call(
        functools.partial(sides_kernel, da, dg, h),
        (shape((RING, *pair), bf16), shape(pair, f32), shape((4, *pair), bf16)),
        work, *ring, inverse, inverse_c, inverse_z, inverse_zc,
        scratch=[pltpu.VMEM((4, *pair), f32)],
    )
    col = jnp.stack([col, swap(after(col, send), "w")])
    got = lax.all_to_all(send, X, 0, 0, tiled=True)
    keep, send = call(
        functools.partial(first_sum_kernel, da),
        (shape(pair, f32), shape((2 * dg + da, block), bf16)),
        0, own, got,
    )
    col = after(col, send)
    cols = [shift(col, X, 4, i + 1) for i in range(3)]
    left, right = call(
        functools.partial(second_sum_kernel, da),
        (shape((da, block), bf16), shape((2, dg, block), bf16)),
        0, keep, swap(send, "w"),
    )
    i_own, g_own, f_keep, f_send = call(
        functools.partial(factor_kernel, da, dg, h, (1.0 - decay_rate) / tokens),
        (shape((da, da * h), f32), shape((dg, dg * h), f32), shape(pack, f32), shape((2, *pack), bf16)),
        work, after(rows, left), col, *cols, input_prior.T, gradient_prior.T,
        scratch=[pltpu.VMEM((4, *pair), bf16)],
    )
    piece = lax.ppermute(left, AXES, piece_perm())
    rights = [shift(right, X, 4, i + 1) for i in range(3)]

    f_got = swap(f_send, "core")
    f_mid = (f_keep + f_got[1].astype(f32)).astype(bf16)
    lefts = lax.all_to_all(jnp.broadcast_to(after(piece, *rights[:2]), (16, *piece.shape)), ("zg", "y"), 0, 0, tiled=True)
    f_last = swap(f_mid, "p")
    input_factor, gradient_factor = call(
        functools.partial(factor_sum_kernel, da, dg, h),
        (shape((da, da * h), f32), shape((dg, dg * h), f32)),
        0, i_own, g_own, f_got, f_last,
    )

    p_own, p_keep, p_send = call(
        functools.partial(product_kernel, h, 1.0 / tokens),
        (shape((da * h, dg), f32), shape((da * h, dg), f32), shape((2, da * h, dg), bf16)),
        2 * tokens * h * da * dg, lefts, right, *rights,
        scratch=[pltpu.VMEM((4, 2, dg, block), bf16)],
    )
    p_got = after(swap(p_send, "core"), f_last)
    p_last = swap((p_keep + p_got[1].astype(f32)).astype(bf16), "p")
    preconditioned = (p_own + p_got[0].astype(f32) + p_last.astype(f32)).astype(bf16)
    return input_factor.T, gradient_factor.T, preconditioned


def solution(mesh):
    split = Mesh(mesh.devices.reshape(SIZES), AXES)
    placed = P(("xh", "xl", "w", "core"), ("zg", "p", "y"))
    return jax.shard_map(
        local,
        mesh=split,
        in_specs=(placed,) * 6,
        out_specs=(placed,) * 3,
        check_vma=False,
    )
```

```python
import functools
import jax
import jax.numpy as jnp
from jax import lax
from jax.experimental import pallas as pl
from jax.experimental.pallas import tpu as pltpu
from jax.sharding import Mesh, PartitionSpec as P

decay_rate = 0.95
VMEM = pl.BlockSpec(memory_space=pltpu.VMEM)
f32, bf16 = jnp.float32, jnp.bfloat16
shape = jax.ShapeDtypeStruct
AXES = ("zg", "p", "y", "xh", "xl", "w", "core")
SIZES = (2, 2, 8, 2, 2, 2, 2)
X = ("xh", "xl")
PANELS = 4
RING = 8


def device(zg, p, y, xh, xl, w, core):
    n = 0
    for size, at in zip(SIZES, (zg, p, y, xh, xl, w, core)):
        n = n * size + at
    return n


def coordinates():
    for n in range(512):
        out = []
        for size in SIZES[::-1]:
            out.append(n % size)
            n //= size
        yield out[::-1]


def panel_perm(flip):
    return [
        (
            device(zg, p, y, xh, xl, w, core),
            device(xh ^ flip, w, PANELS * (xl ^ zg) + y % PANELS, zg, p, y // PANELS, core),
        )
        for zg, p, y, xh, xl, w, core in coordinates()
    ]


def piece_perm():
    return [
        (
            device(zg, p, y, xh, xl, w, core),
            device(xh, p, PANELS * (xl ^ zg) + y % PANELS, zg, w, y // PANELS, core),
        )
        for zg, p, y, xh, xl, w, core in coordinates()
    ]


def column_perm():
    return [
        (
            device(zg, p, y, xh, xl, w, core),
            device(zg, w, y, xh, xl, p, core),
        )
        for zg, p, y, xh, xl, w, core in coordinates()
    ]


def swap(x, axis):
    return lax.ppermute(x, axis, [(0, 1), (1, 0)])


def shift(x, axis, size, by):
    return lax.ppermute(x, axis, [(i, (i + by) % size) for i in range(size)])


def after(x, *others):
    return lax.optimization_barrier((x, *others))[0]


def dot(a, b, dims):
    return lax.dot_general(a, b, (dims, ((), ())), preferred_element_type=f32)


def call(kernel, out, flops, *args, scratch=()):
    size = sum(a.size * a.dtype.itemsize for a in (*args, *jax.tree.leaves(out)))
    return pl.pallas_call(
        kernel,
        out_shape=out,
        in_specs=[VMEM] * len(args),
        out_specs=jax.tree.map(lambda _: VMEM, out),
        scratch_shapes=list(scratch),
        compiler_params=pltpu.CompilerParams(vmem_limit_bytes=8 * 1024 * 1024),
        cost_estimate=pl.CostEstimate(flops=flops, bytes_accessed=size, transcendentals=0),
    )(*args)


def packed_shape(da, dg, h):
    return dg + da // 2, -(-dg * h // 128) * 128


def small_at(da, dg, h):
    lane = -(-da * h // 128) * 128
    return [
        (slice(i * da // 2, (i + 1) * da // 2), slice(dg, dg + da // 2), slice(i * lane, i * lane + da * h))
        for i in range(2)
    ]


def pack_kernel(small, big, out):
    da, dg = small.shape[0], big.shape[0]
    h = big.shape[1] // dg
    out[...] = jnp.zeros_like(out)
    out[:dg, : big.shape[1]] = big[...]
    for rows, to, lanes in small_at(da, dg, h):
        out[to, lanes] = small[rows, :]


def sides_kernel(da, dg, h, *refs):
    ring, inverses = refs[: RING + 1], refs[RING + 1 : RING + 5]
    rows, own, s1, s2, s3, acc = refs[RING + 5 :]
    core, zg, p, y = (lax.axis_index(a) for a in ("core", "zg", "p", "y"))
    group = lax.axis_index("xh")
    x = 2 * group + lax.axis_index("xl")
    width, n = own.shape[1:]

    def place(offset):
        return lax.bitwise_xor(lax.rem(y + offset + RING, RING), PANELS * group)

    for offset, ref in zip((0, -1, 1, -2, 2, -3, 3), ring):
        at = place(offset)
        for slot in range(2):
            rows[at, lax.bitwise_xor(zg, slot)] = ref[slot]
    for slot in range(2):
        rows[place(4), lax.bitwise_xor(zg, slot)] = ring[RING - 1 + slot][...]
    big = [ref[:dg, : dg * h] for ref in inverses]
    small = [
        jnp.concatenate([ref[at, lanes] for _, at, lanes in small_at(da, dg, h)], 0) for ref in inverses
    ]
    for xl in range(2):

        def panel(first, lo, hi):
            return jnp.concatenate(
                [
                    jnp.concatenate([rows[PANELS * xl + first + m, xh, lo:hi, :] for m in range(h)], 0)
                    for xh in range(2)
                ],
                1,
            )

        for lo, hi, blocks in ((0, da, small), (da, width, big)):
            mine, other = panel(core * h, lo, hi), panel((1 - core) * h, lo, hi)
            for q in range(2):
                total = dot(blocks[2 * q], mine, ((1,), (0,))) + dot(blocks[2 * q + 1], other, ((1,), (0,)))
                for xh in range(2):
                    acc[2 * xh + xl, lax.bitwise_xor(p, q), lo:hi, :] = total[:, xh * n : (xh + 1) * n]
    own[...] = acc[x]
    for ahead, ref in enumerate((s1, s2, s3)):
        ref[...] = acc[lax.rem(x + ahead + 1, 4)].astype(ref.dtype)


def first_sum_kernel(da, own, r1, r2, r3, keep, send):
    w = lax.axis_index("w")
    dg = own.shape[1] - da
    keep[...] = ((own[...] + r1[...].astype(f32)) + r2[...].astype(f32)) + r3[...].astype(f32)
    for t in range(2):
        send[t * dg : (t + 1) * dg, :] = keep[t, da:, :].astype(send.dtype)
    send[2 * dg :, :] = keep[1 - w, :da, :].astype(send.dtype)


def second_sum_kernel(da, keep, got, left, right):
    w = lax.axis_index("w")
    dg = right.shape[1]
    for t in range(2):
        right[t] = (keep[t, da:, :] + got[t * dg : (t + 1) * dg, :].astype(f32)).astype(right.dtype)
    left[...] = (keep[w, :da, :] + got[2 * dg :, :].astype(f32)).astype(left.dtype)


def factor_kernel(da, dg, h, weight, rows, c0, c1, c2, c3, ip, gp, i_own, g_own, keep, send, held):
    core, p, w = (lax.axis_index(a) for a in ("core", "p", "w"))
    x = 2 * lax.axis_index("xh") + lax.axis_index("xl")
    for behind, ref in enumerate((c0, c1, c2, c3)):
        held[lax.rem(x - behind + 4, 4)] = ref[...]
    keep[...] = jnp.zeros_like(keep)
    send[...] = jnp.zeros_like(send)

    def panel(k, lo, hi):
        return jnp.concatenate([rows[PANELS * xl + k, xh, lo:hi, :] for xh in range(2) for xl in range(2)], 1)

    def columns(q, lo, hi):
        return jnp.concatenate([held[token, lax.bitwise_xor(q, w), lo:hi, :] for token in range(4)], 1)

    for lo, hi, prior, own in ((0, da, ip, i_own), (da, da + dg, gp, g_own)):
        n = hi - lo
        here, there = columns(p, lo, hi), columns(1 - p, lo, hi)
        for m in range(h):
            at = slice(m * n, (m + 1) * n)
            parts = [
                weight * dot(c, panel(first * h + m, lo, hi), ((1,), (1,)))
                for first in (core, 1 - core)
                for c in (here, there)
            ]
            own[:, at] = decay_rate * prior[:, at] + parts[0]
            for ref, part in ((keep, parts[1]), (send.at[0], parts[2]), (send.at[1], parts[3])):
                if lo:
                    ref[:dg, at] = part.astype(ref.dtype)
                else:
                    for src, to, lanes in small_at(da, dg, h):
                        lane = slice(lanes.start + m * n, lanes.start + (m + 1) * n)
                        ref[to, lane] = part[src, :].astype(ref.dtype)


def factor_sum_kernel(da, dg, h, i_own, g_own, got, last, i_out, g_out):
    def total(at, lanes):
        return got[0, at, lanes].astype(f32) + last[at, lanes].astype(f32)

    g_out[...] = g_own[...] + total(slice(0, dg), slice(0, dg * h))
    for src, at, lanes in small_at(da, dg, h):
        i_out[src, :] = i_own[src, :] + total(at, lanes)


def product_kernel(h, scale, left, right, r1, r2, r3, own, keep, send, held):
    core, p, group = (lax.axis_index(a) for a in ("core", "p", "xh"))
    x = 2 * group + lax.axis_index("xl")
    n = left.shape[1]
    for behind, ref in enumerate((right, r1, r2, r3)):
        held[lax.rem(x - behind + 4, 4)] = ref[...]

    def columns(q):
        return jnp.concatenate([held[token, q] for token in range(4)], 1)

    def panel(k):
        return jnp.concatenate(
            [left[2 * PANELS * xh + PANELS * lax.bitwise_xor(xl, group) + k] for xh in range(2) for xl in range(2)], 1
        )

    here, there = columns(p), columns(1 - p)
    for first, outs in ((1 - core, (send.at[0], send.at[1])), (core, (own, keep))):
        for m in range(h):
            part = panel(first * h + m)
            for c, ref in zip((here, there), outs):
                ref[m * n : (m + 1) * n, :] = (dot(part, c, ((1,), (1,))) * scale).astype(ref.dtype)


def local(activations, output_grads, input_prior, gradient_prior, input_inverse, gradient_inverse):
    da, dg = activations.shape[1], output_grads.shape[1]
    width, block = da + dg, activations.shape[0]
    h = input_prior.shape[0] // da
    tokens = block * 16
    work = 2 * tokens * h * (da * da + dg * dg)
    pair = (2, width, block)
    pack = packed_shape(da, dg, h)

    x = jnp.concatenate([activations.T, output_grads.T], 0)
    inverse = call(pack_kernel, shape(pack, bf16), 0, after(input_inverse.T, x), gradient_inverse.T)
    first, second, col, inverse_c = lax.optimization_barrier(
        (
            lax.ppermute(x, AXES, panel_perm(0)),
            lax.ppermute(x, AXES, panel_perm(1)),
            lax.ppermute(x, AXES, column_perm()),
            swap(inverse, "core"),
        )
    )
    u = jnp.stack([first, second])
    inverse_z = swap(after(inverse, u), "p")
    up, down = [u], [u]
    for stage in range(3):
        if stage == 2:
            col = jnp.stack([col, swap(col, "w")])
            up[2], down[2], col = lax.optimization_barrier((up[2], down[2], col))
        up.append(shift(up[-1], "y", RING, 1))
        down.append(shift(down[-1], "y", RING, -1))
    cols = [shift(col, X, 4, i + 1) for i in range(3)]
    halves = lax.optimization_barrier((up[3][0], down[3][1], *cols))
    cols = list(halves[2:])
    ring = [u, up[1], down[1], up[2], down[2], up[3], down[3]]
    ring += [shift(halves[0], "y", RING, 1), shift(halves[1], "y", RING, -1)]
    inverse_zc = swap(inverse_z, "core")

    rows, own, *ahead = call(
        functools.partial(sides_kernel, da, dg, h),
        (shape((RING, *pair), bf16), shape(pair, f32)) + (shape(pair, bf16),) * 3,
        work, *ring, inverse, inverse_c, inverse_z, inverse_zc,
        scratch=[pltpu.VMEM((4, *pair), f32)],
    )
    got = [shift(part, X, 4, i + 1) for i, part in enumerate(ahead)]
    keep, send = call(
        functools.partial(first_sum_kernel, da),
        (shape(pair, f32), shape((2 * dg + da, block), bf16)),
        0, own, *got,
    )
    left, right = call(
        functools.partial(second_sum_kernel, da),
        (shape((da, block), bf16), shape((2, dg, block), bf16)),
        0, keep, swap(send, "w"),
    )
    i_own, g_own, f_keep, f_send = call(
        functools.partial(factor_kernel, da, dg, h, (1.0 - decay_rate) / tokens),
        (shape((da, da * h), f32), shape((dg, dg * h), f32), shape(pack, f32), shape((2, *pack), bf16)),
        work, rows, col, *cols, input_prior.T, gradient_prior.T,
        scratch=[pltpu.VMEM((4, *pair), bf16)],
    )
    piece = lax.ppermute(left, AXES, piece_perm())
    rights = [shift(right, X, 4, i + 1) for i in range(3)]

    f_got = swap(after(f_send, send), "core")
    f_mid = after((f_keep + f_got[1].astype(f32)).astype(bf16), left)
    f_last = swap(f_mid, "p")
    pieces = jnp.broadcast_to(after(piece, *rights, f_last), (16, *piece.shape))
    lefts = lax.all_to_all(pieces, ("zg", "y"), 0, 0, tiled=True)

    input_factor, gradient_factor = call(
        functools.partial(factor_sum_kernel, da, dg, h),
        (shape((da, da * h), f32), shape((dg, dg * h), f32)),
        0, after(i_own, lefts), g_own, f_got, f_last,
    )
    p_own, p_keep, p_send = call(
        functools.partial(product_kernel, h, 1.0 / tokens),
        (shape((da * h, dg), f32), shape((da * h, dg), f32), shape((2, da * h, dg), bf16)),
        2 * tokens * h * da * dg, lefts, right, *rights,
        scratch=[pltpu.VMEM((4, 2, dg, block), bf16)],
    )
    p_got = swap(p_send, "core")
    p_last = swap((p_keep + p_got[1].astype(f32)).astype(bf16), "p")
    preconditioned = (p_own + p_got[0].astype(f32) + p_last.astype(f32)).astype(bf16)
    return input_factor.T, gradient_factor.T, preconditioned


def solution(mesh):
    split = Mesh(mesh.devices.reshape(SIZES), AXES)
    placed = P(("xh", "xl", "w", "core"), ("zg", "p", "y"))
    return jax.shard_map(
        local,
        mesh=split,
        in_specs=(placed,) * 6,
        out_specs=(placed,) * 3,
        check_vma=False,
    )
```

```python
import functools
import jax
import jax.numpy as jnp
from jax import lax
from jax.experimental import pallas as pl
from jax.experimental.pallas import tpu as pltpu
from jax.sharding import Mesh, PartitionSpec as P

decay_rate = 0.95
VMEM = pl.BlockSpec(memory_space=pltpu.VMEM)
f32, bf16 = jnp.float32, jnp.bfloat16
shape = jax.ShapeDtypeStruct
AXES = ("zg", "p", "y", "xh", "xl", "w", "core")
SIZES = (2, 2, 8, 2, 2, 2, 2)
X = ("xh", "xl")
PANELS = 4
RING = 8


def device(zg, p, y, xh, xl, w, core):
    n = 0
    for size, at in zip(SIZES, (zg, p, y, xh, xl, w, core)):
        n = n * size + at
    return n


def coordinates():
    for n in range(512):
        out = []
        for size in SIZES[::-1]:
            out.append(n % size)
            n //= size
        yield out[::-1]


def panel_perm(flip):
    return [
        (
            device(zg, p, y, xh, xl, w, core),
            device(xh ^ flip, w, PANELS * (xl ^ zg) + y % PANELS, zg, p, y // PANELS, core),
        )
        for zg, p, y, xh, xl, w, core in coordinates()
    ]


def piece_perm():
    return [
        (
            device(zg, p, y, xh, xl, w, core),
            device(xh, p, PANELS * (xl ^ zg) + y % PANELS, zg, w, y // PANELS, core),
        )
        for zg, p, y, xh, xl, w, core in coordinates()
    ]


def column_perm(flip):
    return [
        (
            device(zg, p, y, xh, xl, w, core),
            device(zg, w, y, xh, xl, p ^ flip, core),
        )
        for zg, p, y, xh, xl, w, core in coordinates()
    ]


def swap(x, axis):
    return lax.ppermute(x, axis, [(0, 1), (1, 0)])


def shift(x, axis, size, by):
    return lax.ppermute(x, axis, [(i, (i + by) % size) for i in range(size)])


def after(x, *others):
    return lax.optimization_barrier((x, *others))[0]


def dot(a, b, dims):
    return lax.dot_general(a, b, (dims, ((), ())), preferred_element_type=f32)


def call(kernel, out, flops, *args, scratch=()):
    size = sum(a.size * a.dtype.itemsize for a in (*args, *jax.tree.leaves(out)))
    return pl.pallas_call(
        kernel,
        out_shape=out,
        in_specs=[VMEM] * len(args),
        out_specs=jax.tree.map(lambda _: VMEM, out),
        scratch_shapes=list(scratch),
        compiler_params=pltpu.CompilerParams(vmem_limit_bytes=8 * 1024 * 1024),
        cost_estimate=pl.CostEstimate(flops=flops, bytes_accessed=size, transcendentals=0),
    )(*args)


def packed_shape(da, dg, h):
    return dg + da // 2, -(-dg * h // 128) * 128


def small_at(da, dg, h):
    lane = -(-da * h // 128) * 128
    return [
        (slice(i * da // 2, (i + 1) * da // 2), slice(dg, dg + da // 2), slice(i * lane, i * lane + da * h))
        for i in range(2)
    ]


def pack_kernel(small, big, out):
    da, dg = small.shape[0], big.shape[0]
    h = big.shape[1] // dg
    out[...] = jnp.zeros_like(out)
    out[:dg, : big.shape[1]] = big[...]
    for rows, to, lanes in small_at(da, dg, h):
        out[to, lanes] = small[rows, :]


def sides_kernel(da, dg, h, *refs):
    ring, inverses = refs[: RING + 1], refs[RING + 1 : RING + 5]
    rows, own, s1, s2, s3, acc = refs[RING + 5 :]
    core, zg, p, y = (lax.axis_index(a) for a in ("core", "zg", "p", "y"))
    group = lax.axis_index("xh")
    x = 2 * group + lax.axis_index("xl")
    width, n = own.shape[1:]

    def place(offset):
        return lax.bitwise_xor(lax.rem(y + offset + RING, RING), PANELS * group)

    for offset, ref in zip((0, -1, 1, -2, 2, -3, 3), ring):
        at = place(offset)
        for slot in range(2):
            rows[at, lax.bitwise_xor(zg, slot)] = ref[slot]
    for slot in range(2):
        rows[place(4), lax.bitwise_xor(zg, slot)] = ring[RING - 1 + slot][...]
    big = [ref[:dg, : dg * h] for ref in inverses]
    small = [
        jnp.concatenate([ref[at, lanes] for _, at, lanes in small_at(da, dg, h)], 0) for ref in inverses
    ]
    for xl in range(2):

        def panel(first, lo, hi):
            return jnp.concatenate(
                [
                    jnp.concatenate([rows[PANELS * xl + first + m, xh, lo:hi, :] for m in range(h)], 0)
                    for xh in range(2)
                ],
                1,
            )

        for lo, hi, blocks in ((0, da, small), (da, width, big)):
            mine, other = panel(core * h, lo, hi), panel((1 - core) * h, lo, hi)
            for q in range(2):
                total = dot(blocks[2 * q], mine, ((1,), (0,))) + dot(blocks[2 * q + 1], other, ((1,), (0,)))
                for xh in range(2):
                    acc[2 * xh + xl, lax.bitwise_xor(p, q), lo:hi, :] = total[:, xh * n : (xh + 1) * n]
    own[...] = acc[x]
    for ahead, ref in enumerate((s1, s2, s3)):
        ref[...] = acc[lax.rem(x + ahead + 1, 4)].astype(ref.dtype)


def first_sum_kernel(da, own, r1, r2, r3, keep, send):
    w = lax.axis_index("w")
    dg = own.shape[1] - da
    keep[...] = ((own[...] + r1[...].astype(f32)) + r2[...].astype(f32)) + r3[...].astype(f32)
    for t in range(2):
        send[t * dg : (t + 1) * dg, :] = keep[t, da:, :].astype(send.dtype)
    send[2 * dg :, :] = keep[1 - w, :da, :].astype(send.dtype)


def second_sum_kernel(da, keep, got, left, right):
    w = lax.axis_index("w")
    dg = right.shape[1]
    for t in range(2):
        right[t] = (keep[t, da:, :] + got[t * dg : (t + 1) * dg, :].astype(f32)).astype(right.dtype)
    left[...] = (keep[w, :da, :] + got[2 * dg :, :].astype(f32)).astype(left.dtype)


def factor_kernel(da, dg, h, weight, rows, c0, c1, c2, c3, ip, gp, i_own, g_own, keep, send, held):
    core, p, w = (lax.axis_index(a) for a in ("core", "p", "w"))
    x = 2 * lax.axis_index("xh") + lax.axis_index("xl")
    for behind, ref in enumerate((c0, c1, c2, c3)):
        held[lax.rem(x - behind + 4, 4)] = ref[...]
    keep[...] = jnp.zeros_like(keep)
    send[...] = jnp.zeros_like(send)

    def panel(k, lo, hi):
        return jnp.concatenate([rows[PANELS * xl + k, xh, lo:hi, :] for xh in range(2) for xl in range(2)], 1)

    def columns(q, lo, hi):
        return jnp.concatenate([held[token, lax.bitwise_xor(q, w), lo:hi, :] for token in range(4)], 1)

    for lo, hi, prior, own in ((0, da, ip, i_own), (da, da + dg, gp, g_own)):
        n = hi - lo
        here, there = columns(p, lo, hi), columns(1 - p, lo, hi)
        for m in range(h):
            at = slice(m * n, (m + 1) * n)
            parts = [
                weight * dot(c, panel(first * h + m, lo, hi), ((1,), (1,)))
                for first in (core, 1 - core)
                for c in (here, there)
            ]
            own[:, at] = decay_rate * prior[:, at] + parts[0]
            for ref, part in ((keep, parts[1]), (send.at[0], parts[2]), (send.at[1], parts[3])):
                if lo:
                    ref[:dg, at] = part.astype(ref.dtype)
                else:
                    for src, to, lanes in small_at(da, dg, h):
                        lane = slice(lanes.start + m * n, lanes.start + (m + 1) * n)
                        ref[to, lane] = part[src, :].astype(ref.dtype)


def factor_sum_kernel(da, dg, h, i_own, g_own, got, last, i_out, g_out):
    def total(at, lanes):
        return got[0, at, lanes].astype(f32) + last[at, lanes].astype(f32)

    g_out[...] = g_own[...] + total(slice(0, dg), slice(0, dg * h))
    for src, at, lanes in small_at(da, dg, h):
        i_out[src, :] = i_own[src, :] + total(at, lanes)


def product_kernel(h, scale, left, right, r1, r2, r3, own, keep, send, held):
    core, p, group = (lax.axis_index(a) for a in ("core", "p", "xh"))
    x = 2 * group + lax.axis_index("xl")
    n = left.shape[1]
    for behind, ref in enumerate((right, r1, r2, r3)):
        held[lax.rem(x - behind + 4, 4)] = ref[...]

    def columns(q):
        return jnp.concatenate([held[token, q] for token in range(4)], 1)

    def panel(k):
        return jnp.concatenate(
            [left[2 * PANELS * xh + PANELS * lax.bitwise_xor(xl, group) + k] for xh in range(2) for xl in range(2)], 1
        )

    here, there = columns(p), columns(1 - p)
    for first, outs in ((1 - core, (send.at[0], send.at[1])), (core, (own, keep))):
        for m in range(h):
            part = panel(first * h + m)
            for c, ref in zip((here, there), outs):
                ref[m * n : (m + 1) * n, :] = (dot(part, c, ((1,), (1,))) * scale).astype(ref.dtype)


def local(activations, output_grads, input_prior, gradient_prior, input_inverse, gradient_inverse):
    da, dg = activations.shape[1], output_grads.shape[1]
    width, block = da + dg, activations.shape[0]
    h = input_prior.shape[0] // da
    tokens = block * 16
    work = 2 * tokens * h * (da * da + dg * dg)
    pair = (2, width, block)
    pack = packed_shape(da, dg, h)

    x = jnp.concatenate([activations.T, output_grads.T], 0)
    inverse = call(pack_kernel, shape(pack, bf16), 0, after(input_inverse.T, x), gradient_inverse.T)
    near, far = (lax.ppermute(x, AXES, column_perm(j)) for j in range(2))
    first, second, col, inverse_c, inverse_z = lax.optimization_barrier(
        (
            lax.ppermute(x, AXES, panel_perm(0)),
            lax.ppermute(x, AXES, panel_perm(1)),
            jnp.stack([near, far]),
            swap(inverse, "core"),
            swap(inverse, "p"),
        )
    )
    cols = [shift(col, X, 4, i + 1) for i in range(3)]
    u = jnp.stack([first, second])
    up, down = [u], [u]
    for _ in range(3):
        up.append(shift(up[-1], "y", RING, 1))
        down.append(shift(down[-1], "y", RING, -1))
    ring = [u, up[1], down[1], up[2], down[2], up[3], down[3]]
    ring += [shift(up[3][0], "y", RING, 1), shift(down[3][1], "y", RING, -1)]
    inverse_zc = swap(inverse_z, "core")

    rows, own, *ahead = call(
        functools.partial(sides_kernel, da, dg, h),
        (shape((RING, *pair), bf16), shape(pair, f32)) + (shape(pair, bf16),) * 3,
        work, *ring, inverse, inverse_c, inverse_z, inverse_zc,
        scratch=[pltpu.VMEM((4, *pair), f32)],
    )
    got = [shift(part, X, 4, i + 1) for i, part in enumerate(ahead)]
    keep, send = call(
        functools.partial(first_sum_kernel, da),
        (shape(pair, f32), shape((2 * dg + da, block), bf16)),
        0, own, *got,
    )
    left, right = call(
        functools.partial(second_sum_kernel, da),
        (shape((da, block), bf16), shape((2, dg, block), bf16)),
        0, keep, swap(send, "w"),
    )
    i_own, g_own, f_keep, f_send = call(
        functools.partial(factor_kernel, da, dg, h, (1.0 - decay_rate) / tokens),
        (shape((da, da * h), f32), shape((dg, dg * h), f32), shape(pack, f32), shape((2, *pack), bf16)),
        work, rows, col, *cols, input_prior.T, gradient_prior.T,
        scratch=[pltpu.VMEM((4, *pair), bf16)],
    )
    piece = lax.ppermute(left, AXES, piece_perm())
    rights = [shift(right, X, 4, i + 1) for i in range(3)]

    f_got = swap(after(f_send, send), "core")
    f_mid = after((f_keep + f_got[1].astype(f32)).astype(bf16), left)
    f_last = swap(f_mid, "p")
    pieces = jnp.broadcast_to(after(piece, *rights, f_last), (16, *piece.shape))
    lefts = lax.all_to_all(pieces, ("zg", "y"), 0, 0, tiled=True)

    input_factor, gradient_factor = call(
        functools.partial(factor_sum_kernel, da, dg, h),
        (shape((da, da * h), f32), shape((dg, dg * h), f32)),
        0, after(i_own, lefts), g_own, f_got, f_last,
    )
    p_own, p_keep, p_send = call(
        functools.partial(product_kernel, h, 1.0 / tokens),
        (shape((da * h, dg), f32), shape((da * h, dg), f32), shape((2, da * h, dg), bf16)),
        2 * tokens * h * da * dg, lefts, right, *rights,
        scratch=[pltpu.VMEM((4, 2, dg, block), bf16)],
    )
    p_got = swap(p_send, "core")
    p_last = swap((p_keep + p_got[1].astype(f32)).astype(bf16), "p")
    preconditioned = (p_own + p_got[0].astype(f32) + p_last.astype(f32)).astype(bf16)
    return input_factor.T, gradient_factor.T, preconditioned


def solution(mesh):
    split = Mesh(mesh.devices.reshape(SIZES), AXES)
    placed = P(("xh", "xl", "w", "core"), ("zg", "p", "y"))
    return jax.shard_map(
        local,
        mesh=split,
        in_specs=(placed,) * 6,
        out_specs=(placed,) * 3,
        check_vma=False,
    )
```

```python
import functools
import jax
import jax.numpy as jnp
from jax import lax
from jax.experimental import pallas as pl
from jax.experimental.pallas import tpu as pltpu
from jax.sharding import Mesh, PartitionSpec as P

decay_rate = 0.95
VMEM = pl.BlockSpec(memory_space=pltpu.VMEM)
f32, bf16 = jnp.float32, jnp.bfloat16
shape = jax.ShapeDtypeStruct
AXES = ("zg", "p", "y", "xh", "xl", "w", "core")
SIZES = (2, 2, 8, 2, 2, 2, 2)
X = ("xh", "xl")
PANELS = 4
RING = 8


def device(zg, p, y, xh, xl, w, core):
    n = 0
    for size, at in zip(SIZES, (zg, p, y, xh, xl, w, core)):
        n = n * size + at
    return n


def coordinates():
    for n in range(512):
        out = []
        for size in SIZES[::-1]:
            out.append(n % size)
            n //= size
        yield out[::-1]


def panel_perm(flip):
    return [
        (
            device(zg, p, y, xh, xl, w, core),
            device(xh ^ flip, w, PANELS * (xl ^ zg) + y % PANELS, zg, p, y // PANELS, core),
        )
        for zg, p, y, xh, xl, w, core in coordinates()
    ]


def piece_perm():
    return [
        (
            device(zg, p, y, xh, xl, w, core),
            device(xh, p, PANELS * (xl ^ zg) + y % PANELS, zg, w, y // PANELS, core),
        )
        for zg, p, y, xh, xl, w, core in coordinates()
    ]


def column_perm():
    return [
        (
            device(zg, p, y, xh, xl, w, core),
            device(zg, w, y, xh, xl, p, core),
        )
        for zg, p, y, xh, xl, w, core in coordinates()
    ]


def swap(x, axis):
    return lax.ppermute(x, axis, [(0, 1), (1, 0)])


def shift(x, axis, size, by):
    return lax.ppermute(x, axis, [(i, (i + by) % size) for i in range(size)])


def after(x, *others):
    return lax.optimization_barrier((x, *others))[0]


def dot(a, b, dims):
    return lax.dot_general(a, b, (dims, ((), ())), preferred_element_type=f32)


def call(kernel, out, flops, *args, scratch=()):
    size = sum(a.size * a.dtype.itemsize for a in (*args, *jax.tree.leaves(out)))
    return pl.pallas_call(
        kernel,
        out_shape=out,
        in_specs=[VMEM] * len(args),
        out_specs=jax.tree.map(lambda _: VMEM, out),
        scratch_shapes=list(scratch),
        compiler_params=pltpu.CompilerParams(vmem_limit_bytes=8 * 1024 * 1024),
        cost_estimate=pl.CostEstimate(flops=flops, bytes_accessed=size, transcendentals=0),
    )(*args)


def packed_shape(da, dg, h):
    return dg + da // 2, -(-dg * h // 128) * 128


def small_at(da, dg, h):
    lane = -(-da * h // 128) * 128
    return [
        (slice(i * da // 2, (i + 1) * da // 2), slice(dg, dg + da // 2), slice(i * lane, i * lane + da * h))
        for i in range(2)
    ]


def pack_kernel(small, big, out):
    da, dg = small.shape[0], big.shape[0]
    h = big.shape[1] // dg
    out[...] = jnp.zeros_like(out)
    out[:dg, : big.shape[1]] = big[...]
    for rows, to, lanes in small_at(da, dg, h):
        out[to, lanes] = small[rows, :]


def sides_kernel(da, dg, h, *refs):
    ring, inverses = refs[: RING + 1], refs[RING + 1 : RING + 5]
    rows, own, s1, s2, s3, acc = refs[RING + 5 :]
    core, zg, p, y = (lax.axis_index(a) for a in ("core", "zg", "p", "y"))
    group = lax.axis_index("xh")
    x = 2 * group + lax.axis_index("xl")
    width, n = own.shape[1:]

    def place(offset):
        return lax.bitwise_xor(lax.rem(y + offset + RING, RING), PANELS * group)

    for offset, ref in zip((0, -1, 1, -2, 2, -3, 3), ring):
        at = place(offset)
        for slot in range(2):
            rows[at, lax.bitwise_xor(zg, slot)] = ref[slot]
    for slot in range(2):
        rows[place(4), lax.bitwise_xor(zg, slot)] = ring[RING - 1 + slot][...]
    big = [ref[:dg, : dg * h] for ref in inverses]
    small = [
        jnp.concatenate([ref[at, lanes] for _, at, lanes in small_at(da, dg, h)], 0) for ref in inverses
    ]
    for xl in range(2):

        def panel(first, lo, hi):
            return jnp.concatenate(
                [
                    jnp.concatenate([rows[PANELS * xl + first + m, xh, lo:hi, :] for m in range(h)], 0)
                    for xh in range(2)
                ],
                1,
            )

        for lo, hi, blocks in ((0, da, small), (da, width, big)):
            mine, other = panel(core * h, lo, hi), panel((1 - core) * h, lo, hi)
            for q in range(2):
                total = dot(blocks[2 * q], mine, ((1,), (0,))) + dot(blocks[2 * q + 1], other, ((1,), (0,)))
                for xh in range(2):
                    acc[2 * xh + xl, lax.bitwise_xor(p, q), lo:hi, :] = total[:, xh * n : (xh + 1) * n]
    own[...] = acc[x]
    for ahead, ref in enumerate((s1, s2, s3)):
        ref[...] = acc[lax.rem(x + ahead + 1, 4)].astype(ref.dtype)


def first_sum_kernel(da, own, r1, r2, r3, keep, send):
    w = lax.axis_index("w")
    dg = own.shape[1] - da
    keep[...] = ((own[...] + r1[...].astype(f32)) + r2[...].astype(f32)) + r3[...].astype(f32)
    for t in range(2):
        send[t * dg : (t + 1) * dg, :] = keep[t, da:, :].astype(send.dtype)
    send[2 * dg :, :] = keep[1 - w, :da, :].astype(send.dtype)


def second_sum_kernel(da, keep, got, left, right):
    w = lax.axis_index("w")
    dg = right.shape[1]
    for t in range(2):
        right[t] = (keep[t, da:, :] + got[t * dg : (t + 1) * dg, :].astype(f32)).astype(right.dtype)
    left[...] = (keep[w, :da, :] + got[2 * dg :, :].astype(f32)).astype(left.dtype)


def factor_kernel(da, dg, h, weight, rows, c0, c1, c2, c3, ip, gp, i_own, g_own, keep, send, held):
    core, p, w = (lax.axis_index(a) for a in ("core", "p", "w"))
    x = 2 * lax.axis_index("xh") + lax.axis_index("xl")
    for behind, ref in enumerate((c0, c1, c2, c3)):
        held[lax.rem(x - behind + 4, 4)] = ref[...]
    keep[...] = jnp.zeros_like(keep)
    send[...] = jnp.zeros_like(send)

    def panel(k, lo, hi):
        return jnp.concatenate([rows[PANELS * xl + k, xh, lo:hi, :] for xh in range(2) for xl in range(2)], 1)

    def columns(q, lo, hi):
        return jnp.concatenate([held[token, lax.bitwise_xor(q, w), lo:hi, :] for token in range(4)], 1)

    for lo, hi, prior, own in ((0, da, ip, i_own), (da, da + dg, gp, g_own)):
        n = hi - lo
        here, there = columns(p, lo, hi), columns(1 - p, lo, hi)
        for m in range(h):
            at = slice(m * n, (m + 1) * n)
            parts = [
                weight * dot(c, panel(first * h + m, lo, hi), ((1,), (1,)))
                for first in (core, 1 - core)
                for c in (here, there)
            ]
            own[:, at] = decay_rate * prior[:, at] + parts[0]
            for ref, part in ((keep, parts[1]), (send.at[0], parts[2]), (send.at[1], parts[3])):
                if lo:
                    ref[:dg, at] = part.astype(ref.dtype)
                else:
                    for src, to, lanes in small_at(da, dg, h):
                        lane = slice(lanes.start + m * n, lanes.start + (m + 1) * n)
                        ref[to, lane] = part[src, :].astype(ref.dtype)


def factor_sum_kernel(da, dg, h, i_own, g_own, got, last, i_out, g_out):
    def total(at, lanes):
        return got[0, at, lanes].astype(f32) + last[at, lanes].astype(f32)

    g_out[...] = g_own[...] + total(slice(0, dg), slice(0, dg * h))
    for src, at, lanes in small_at(da, dg, h):
        i_out[src, :] = i_own[src, :] + total(at, lanes)


def product_kernel(h, scale, left, right, r1, r2, r3, own, keep, send, held):
    core, p, group = (lax.axis_index(a) for a in ("core", "p", "xh"))
    x = 2 * group + lax.axis_index("xl")
    n = left.shape[1]
    for behind, ref in enumerate((right, r1, r2, r3)):
        held[lax.rem(x - behind + 4, 4)] = ref[...]

    def columns(q):
        return jnp.concatenate([held[token, q] for token in range(4)], 1)

    def panel(k):
        return jnp.concatenate(
            [left[2 * PANELS * xh + PANELS * lax.bitwise_xor(xl, group) + k] for xh in range(2) for xl in range(2)], 1
        )

    here, there = columns(p), columns(1 - p)
    for first, outs in ((1 - core, (send.at[0], send.at[1])), (core, (own, keep))):
        for m in range(h):
            part = panel(first * h + m)
            for c, ref in zip((here, there), outs):
                ref[m * n : (m + 1) * n, :] = (dot(part, c, ((1,), (1,))) * scale).astype(ref.dtype)


def local(activations, output_grads, input_prior, gradient_prior, input_inverse, gradient_inverse):
    da, dg = activations.shape[1], output_grads.shape[1]
    width, block = da + dg, activations.shape[0]
    h = input_prior.shape[0] // da
    tokens = block * 16
    work = 2 * tokens * h * (da * da + dg * dg)
    pair = (2, width, block)
    pack = packed_shape(da, dg, h)

    x = jnp.concatenate([activations.T, output_grads.T], 0)
    inverse = call(pack_kernel, shape(pack, bf16), 0, after(input_inverse.T, x), gradient_inverse.T)
    first, second, col, inverse_c, inverse_z = lax.optimization_barrier(
        (
            lax.ppermute(x, AXES, panel_perm(0)),
            lax.ppermute(x, AXES, panel_perm(1)),
            lax.ppermute(x, AXES, column_perm()),
            swap(inverse, "core"),
            swap(inverse, "p"),
        )
    )
    u = jnp.stack([first, second])
    up, down = [u], [u]
    for _ in range(3):
        up.append(shift(up[-1], "y", RING, 1))
        down.append(shift(down[-1], "y", RING, -1))
    ring = [u, up[1], down[1], up[2], down[2], up[3], down[3]]
    ring += [shift(up[3][0], "y", RING, 1), shift(down[3][1], "y", RING, -1)]

    inverse_zc = swap(inverse_z, "core")
    col = jnp.stack([col, swap(after(col, up[1], down[1]), "w")])
    cols = [shift(col, X, 4, i + 1) for i in range(3)]

    rows, own, *ahead = call(
        functools.partial(sides_kernel, da, dg, h),
        (shape((RING, *pair), bf16), shape(pair, f32)) + (shape(pair, bf16),) * 3,
        work, *ring, inverse, inverse_c, inverse_z, inverse_zc,
        scratch=[pltpu.VMEM((4, *pair), f32)],
    )
    got = [shift(part, X, 4, i + 1) for i, part in enumerate(ahead)]
    keep, send = call(
        functools.partial(first_sum_kernel, da),
        (shape(pair, f32), shape((2 * dg + da, block), bf16)),
        0, own, *got,
    )
    left, right = call(
        functools.partial(second_sum_kernel, da),
        (shape((da, block), bf16), shape((2, dg, block), bf16)),
        0, keep, swap(send, "w"),
    )
    i_own, g_own, f_keep, f_send = call(
        functools.partial(factor_kernel, da, dg, h, (1.0 - decay_rate) / tokens),
        (shape((da, da * h), f32), shape((dg, dg * h), f32), shape(pack, f32), shape((2, *pack), bf16)),
        work, rows, col, *cols, input_prior.T, gradient_prior.T,
        scratch=[pltpu.VMEM((4, *pair), bf16)],
    )
    piece = lax.ppermute(left, AXES, piece_perm())
    rights = [shift(right, X, 4, i + 1) for i in range(3)]

    f_got = swap(after(f_send, send), "core")
    f_mid = after((f_keep + f_got[1].astype(f32)).astype(bf16), left)
    f_last = swap(f_mid, "p")
    pieces = jnp.broadcast_to(piece, (16, *piece.shape))
    lefts = lax.all_to_all(pieces, ("zg", "y"), 0, 0, tiled=True)
    input_factor, gradient_factor = call(
        functools.partial(factor_sum_kernel, da, dg, h),
        (shape((da, da * h), f32), shape((dg, dg * h), f32)),
        0, i_own, g_own, f_got, f_last,
    )

    p_own, p_keep, p_send = call(
        functools.partial(product_kernel, h, 1.0 / tokens),
        (shape((da * h, dg), f32), shape((da * h, dg), f32), shape((2, da * h, dg), bf16)),
        2 * tokens * h * da * dg, lefts, right, *rights,
        scratch=[pltpu.VMEM((4, 2, dg, block), bf16)],
    )
    p_got = after(swap(p_send, "core"), f_last)
    p_last = swap((p_keep + p_got[1].astype(f32)).astype(bf16), "p")
    preconditioned = (p_own + p_got[0].astype(f32) + p_last.astype(f32)).astype(bf16)
    return input_factor.T, gradient_factor.T, preconditioned


def solution(mesh):
    split = Mesh(mesh.devices.reshape(SIZES), AXES)
    placed = P(("xh", "xl", "w", "core"), ("zg", "p", "y"))
    return jax.shard_map(
        local,
        mesh=split,
        in_specs=(placed,) * 6,
        out_specs=(placed,) * 3,
        check_vma=False,
    )
```
